512 devices in a mesh: slab: 64 (over y_hi, z, core), head: 8 (over y_lo, x).
Axes of the slice: x: 4, y: 4 (y_hi: 2, y_lo: 2; y = y_hi * 2 + y_lo), z: 16, core: 2. Of those that a mesh axis runs over, the one named last changes fastest.
Arguments:
- q_vals: bfloat16 [51200, 3072], P(('slab', 'head')), may hold values from -72 to 72
- k_vals: bfloat16 [51200, 3072], P(('slab', 'head')), may hold values from -6 to 6
- v_vals: bfloat16 [51200, 3072], P(('slab', 'head')), may hold values from -6 to 6
- q_scale: bfloat16 [51200, 24], P(('slab', 'head')), may hold values from 0.25 to 2.5
- k_scale: bfloat16 [51200, 24], P(('slab', 'head')), may hold values from 0.25 to 2.5
- v_scale: bfloat16 [51200, 24], P(('slab', 'head')), may hold values from 0.25 to 2.5
- window: int32 [24, 3], replicated, may hold values from 0 to 2, as said below
Outputs:
- attended: bfloat16 [51200, 3072], P(('slab', 'head'))
The draws below stay inside these ranges and needn't reach their ends.
Inputs may be any that keep to these rules, and one draw needn't show every extreme that they name: window[h, 0] and window[h, 1] are 0 or 1; window[h, 2] is 0, 1 or 2.
All inputs are finite; a program needn't handle non-finite values.
Results may differ from the reference program's by a relative error of at most 0.011.
Values may be sent and summed in bfloat16 or wider, within the bound.
No kernel may reach another device: no remote copies, remote signals or barrier semaphores. Data moves between devices by JAX's collectives and lax.ppermute only.
A program may use at most 64 MiB of HBM per device.

```python
import math
import jax
import jax.numpy as jnp
from jax import lax

HEADS = 24
HEAD_DIM = 128
D = 3072
SF = 1
TILE_H = 5
TILE_W = 8
FRAME_W = 80
FRAME = 800
FRAMES = 64
TOKENS = 51200


def shared_rows(key):
    return jnp.clip(jax.random.normal(key, (TOKENS, D), jnp.float32), -6.0, 6.0)


def draw_k_vals(key, part):
    base = shared_rows(key)
    return base.astype(jnp.bfloat16)


def draw_q_vals(key, part):
    key = jax.random.fold_in(key, 1)
    own = jnp.clip(jax.random.normal(key, (TOKENS, D), jnp.float32), -6.0, 6.0)
    result = own
    return result.astype(jnp.bfloat16)


def draw_window(key, part):
    key = jax.random.fold_in(key, 3)
    key_frame, key_row, key_col = jax.random.split(key, 3)
    frame_reach = jax.random.randint(key_frame, (HEADS, 1), 0, 2, jnp.int32)
    row_reach = jax.random.randint(key_row, (HEADS, 1), 0, 2, jnp.int32)
    col_reach = jax.random.randint(key_col, (HEADS, 1), 0, 3, jnp.int32)
    return jnp.concatenate([frame_reach, row_reach, col_reach], 1)


def steps_of(key, extent, cuts, low, largest):
    def one(axis_at, shards_of):
        steps = jax.random.uniform(jax.random.fold_in(jax.random.fold_in(key, 6), axis_at), (shards_of,), jnp.float32, low / len(cuts), largest / len(cuts))
        return jnp.repeat(jnp.exp(steps), extent[axis_at] // shards_of).reshape((-1,) + (1,) * (len(extent) - axis_at - 1))

    loudness = one(*cuts[0])
    for cut in cuts[1:]:
        loudness = loudness * one(*cut)
    return loudness


def normal_values(own_key, dims, spread, bound, pieces=(), kind=jnp.bfloat16):
    array = jax.random.normal(own_key, dims, jnp.float32) * spread
    if len(pieces) > 0:
        array = steps_of(own_key, dims, pieces, -0.22, 0.18) * array
    return jnp.clip(array, min=-bound, max=bound).astype(kind)


def setup_inputs(seed: int = 0) -> dict:
    arg_keys = jax.random.split(jax.random.key(seed), 8)
    q_vals = draw_q_vals(jax.random.fold_in(arg_keys[7], 71), 0)
    k_vals = draw_k_vals(jax.random.fold_in(arg_keys[7], 71), 0)
    v_vals = normal_values(arg_keys[2], (TOKENS, D), 1.0, 6.0, ((0, 512),))
    q_scale = jnp.clip(jnp.exp(math.log(2.5) - 2.3025851 * jax.random.uniform(arg_keys[3], (TOKENS, HEADS), jnp.float32) ** steps_of(arg_keys[3], (TOKENS, HEADS), ((0, 512),), -0.2, 0.2)), 0.25, 2.5).astype(jnp.bfloat16)
    k_scale = jnp.clip(jnp.exp(math.log(2.5) - 2.3025851 * jax.random.uniform(arg_keys[4], (TOKENS, HEADS), jnp.float32) ** steps_of(arg_keys[4], (TOKENS, HEADS), ((0, 512),), -0.2, 0.2)), 0.25, 2.5).astype(jnp.bfloat16)
    v_scale = jnp.clip(jnp.exp(math.log(2.5) - 2.3025851 * jax.random.uniform(arg_keys[5], (TOKENS, HEADS), jnp.float32) ** steps_of(arg_keys[5], (TOKENS, HEADS), ((0, 512),), -0.2, 0.2)), 0.25, 2.5).astype(jnp.bfloat16)
    window = draw_window(jax.random.fold_in(arg_keys[7], 71), 0)
    return dict(q_vals=q_vals, k_vals=k_vals, v_vals=v_vals, q_scale=q_scale, k_scale=k_scale, v_scale=v_scale, window=window)


def dequant(vals, scales):
    wide = vals.reshape(TOKENS, HEADS, HEAD_DIM).astype(jnp.float32) * scales.astype(jnp.float32)[:, :, None]
    return wide.astype(jnp.bfloat16).reshape(FRAMES, FRAME, HEADS, HEAD_DIM)


def reference(q_vals, k_vals, v_vals, q_scale, k_scale, v_scale, window):
    q_deq = dequant(q_vals, q_scale)
    k_deq = dequant(k_vals, k_scale)
    v_deq = dequant(v_vals, v_scale)
    blank = jnp.zeros((SF, FRAME, HEADS, HEAD_DIM), jnp.bfloat16)
    k_pad = jnp.concatenate([blank, k_deq, blank], 0)
    v_pad = jnp.concatenate([blank, v_deq, blank], 0)
    span = 2 * SF + 1
    places = jnp.arange(FRAME, dtype=jnp.int32)
    tile_row = (places // FRAME_W) // TILE_H
    tile_col = (places % FRAME_W) // TILE_W
    key_row = jnp.tile(tile_row, span)
    key_col = jnp.tile(tile_col, span)
    key_frame = jnp.repeat(jnp.arange(span, dtype=jnp.int32), FRAME)
    row_gap = jnp.abs(tile_row[:, None] - key_row[None, :])
    col_gap = jnp.abs(tile_col[:, None] - key_col[None, :])
    frame_gap = jnp.abs(key_frame - SF)
    scale = 1.0 / (HEAD_DIM ** 0.5)

    def one_frame(frame_id):
        queries = q_deq[frame_id].astype(jnp.float32)
        start = frame_id.astype(jnp.int32)
        zero = jnp.zeros((), jnp.int32)
        keys = lax.dynamic_slice(k_pad, (start, zero, zero, zero), (span, FRAME, HEADS, HEAD_DIM))
        values = lax.dynamic_slice(v_pad, (start, zero, zero, zero), (span, FRAME, HEADS, HEAD_DIM))
        keys = keys.reshape(span * FRAME, HEADS, HEAD_DIM).astype(jnp.float32)
        values = values.reshape(span * FRAME, HEADS, HEAD_DIM).astype(jnp.float32)
        scores = jnp.einsum("qhd,khd->hqk", queries, keys) * scale
        key_global = start - SF + key_frame
        inside = (key_global >= 0) & (key_global < FRAMES)
        allowed = (frame_gap[None, None, :] <= window[:, 0][:, None, None])
        allowed = allowed & (row_gap[None] <= window[:, 1][:, None, None])
        allowed = allowed & (col_gap[None] <= window[:, 2][:, None, None])
        allowed = allowed & inside[None, None, :]
        masked = jnp.where(allowed, scores, -1e30)
        top = jnp.max(masked, axis=-1, keepdims=True)
        expd = jnp.exp(masked - top)
        probs = expd / jnp.sum(expd, axis=-1, keepdims=True)
        weights = probs.astype(jnp.bfloat16).astype(jnp.float32)
        result = jnp.einsum("hqk,khd->qhd", weights, values)
        return result.astype(jnp.bfloat16).reshape(FRAME, D)

    attended = lax.map(one_frame, jnp.arange(FRAMES, dtype=jnp.int32))
    return attended.reshape(TOKENS, D)
```

```python
import functools

import jax
import jax.numpy as jnp
from jax import lax
from jax.experimental import pallas as pl
from jax.experimental.pallas import tpu as pltpu
from jax.sharding import PartitionSpec as P

TILE_H = 5
TILE_W = 8
FRAME_W = 80
HEAD_DIM = 128
MASKED = -1e30


def geometry(tokens):
    rows = tokens // FRAME_W
    return rows, FRAME_W // TILE_W, rows * TILE_W


def padded(rows):
    return -(-rows // 8) * 8


def pack_kernel(flip_ref, *refs, groups):
    count = (len(refs) - 1) // 2
    out_ref = refs[-1]
    rows = refs[0].shape[0]
    width = refs[0].shape[1] // groups
    heads = width // HEAD_DIM
    slot_rows = out_ref.shape[1]
    blank = jnp.zeros((slot_rows - rows, HEAD_DIM), jnp.float32)
    for at in range(count):
        vals_ref, scale_ref = refs[2 * at], refs[2 * at + 1]
        scales = scale_ref[...].astype(jnp.float32)
        for group in range(groups):
            slot = group ^ flip_ref[0]
            for head in range(heads):
                index = group * heads + head
                vals = vals_ref[:, index * HEAD_DIM : (index + 1) * HEAD_DIM]
                wide = vals.astype(jnp.float32) * scales[:, index : index + 1]
                if slot_rows > rows:
                    wide = jnp.concatenate([wide, blank], 0)
                low = at * width + head * HEAD_DIM
                out_ref[slot, :, low : low + HEAD_DIM] = wide.astype(jnp.bfloat16)


def pack(flip, pairs, groups):
    rows, full = pairs[0][0].shape
    width = full // groups
    vmem = pl.BlockSpec(memory_space=pltpu.VMEM)
    return pl.pallas_call(
        functools.partial(pack_kernel, groups=groups),
        out_shape=jax.ShapeDtypeStruct(
            (groups, padded(rows), width * len(pairs)), jnp.bfloat16
        ),
        in_specs=[pl.BlockSpec(memory_space=pltpu.SMEM)] + [vmem] * (2 * len(pairs)),
        out_specs=vmem,
        compiler_params=pltpu.CompilerParams(vmem_limit_bytes=32 * 2**20),
        cost_estimate=pl.CostEstimate(
            flops=rows * full * len(pairs),
            bytes_accessed=4 * rows * full * len(pairs),
            transcendentals=0,
        ),
    )(flip, *[ref for pair in pairs for ref in pair])


def unpack_kernel(flip_ref, in_ref, out_ref):
    groups, _, width = in_ref.shape
    rows = out_ref.shape[0]
    for group in range(groups):
        slot = in_ref[group ^ flip_ref[0]]
        out_ref[:, group * width : (group + 1) * width] = slot[:rows]


def unpack(flip, slots, rows):
    groups, _, width = slots.shape
    vmem = pl.BlockSpec(memory_space=pltpu.VMEM)
    return pl.pallas_call(
        unpack_kernel,
        out_shape=jax.ShapeDtypeStruct((rows, groups * width), jnp.bfloat16),
        in_specs=[pl.BlockSpec(memory_space=pltpu.SMEM), vmem],
        out_specs=vmem,
        compiler_params=pltpu.CompilerParams(vmem_limit_bytes=32 * 2**20),
    )(flip, slots)


def by_columns(slots_ref, lin_ref, chunk):
    slots = slots_ref.shape[0]
    rows, cols, _ = geometry(slots * chunk)
    for slot in range(slots):
        part = slots_ref[slot].astype(jnp.float32)
        lin_ref[slot * chunk : slot * chunk + part.shape[0], :] = part
    for col in range(cols):
        pieces = []
        for row in range(rows):
            low = row * FRAME_W + col * TILE_W
            pieces.append(lin_ref[low : low + TILE_W, :])
        yield col, jnp.concatenate(pieces, 0)


def attend_kernel(meta_ref, q_ref, *refs, chunk, block_cols, reach):
    keys_in, values_in = refs[0:3], refs[3:6]
    out_ref, lin_ref, qs_ref, ks_ref, vs_ref, lin_out_ref = refs[6:]
    slots, slot_rows, _ = q_ref.shape
    rows, cols, strip = geometry(slots * chunk)
    half = strip * TILE_H // rows
    classes = rows // TILE_H
    span = len(keys_in)
    head = pl.program_id(0)
    reach_frame = meta_ref[3 * head]
    reach_row = meta_ref[3 * head + 1]
    reach_col = meta_ref[3 * head + 2]
    first = jnp.where(reach_frame >= 1, meta_ref[meta_ref.shape[0] - 2], 1)
    last = jnp.where(reach_frame >= 1, meta_ref[meta_ref.shape[0] - 1], 1)

    @pl.when(head == 0)
    def _():
        vs_ref[:, HEAD_DIM:] = jnp.ones(
            (vs_ref.shape[0], vs_ref.shape[1] - HEAD_DIM), vs_ref.dtype
        )

    for col, part in by_columns(q_ref, lin_ref, chunk):
        qs_ref[col * strip : (col + 1) * strip, :] = part.astype(jnp.bfloat16)
    for frame in range(span):
        for col, part in by_columns(keys_in[frame], lin_ref, chunk):
            low = (col * span + frame) * strip
            ks_ref[low : low + strip, :] = part.astype(jnp.bfloat16)
        for col, part in by_columns(values_in[frame], lin_ref, chunk):
            low = (col * span + frame) * strip
            vs_ref[low : low + strip, :HEAD_DIM] = part.astype(jnp.bfloat16)

    scale = 1.4426950408889634 / HEAD_DIM**0.5
    for start in range(0, cols, block_cols):
        low_col, high_col = max(0, start - reach), min(cols, start + block_cols + reach)
        keys = (high_col - low_col) * span * strip
        at = lax.broadcasted_iota(jnp.int32, (1, keys), 1).astype(jnp.float32)
        key_col = jnp.floor((at + 0.5) * (1.0 / (span * strip)))
        rest = at - key_col * (span * strip)
        key_frame = jnp.floor((rest + 0.5) * (1.0 / strip))
        rest = rest - key_frame * strip
        key_row = jnp.floor((rest + 0.5) * (1.0 / half))
        frame_ok = (key_frame >= first.astype(jnp.float32)) & (
            key_frame <= last.astype(jnp.float32)
        )
        q_block = qs_ref[start * strip : (start + block_cols) * strip, :]
        key_rows = slice(low_col * span * strip, high_col * span * strip)
        scores = lax.dot_general(
            q_block,
            ks_ref[key_rows, :],
            (((1,), (1,)), ((), ())),
            preferred_element_type=jnp.float32,
        )
        weights = []
        for col in range(start, start + block_cols):
            col_ok = frame_ok & (
                jnp.abs(key_col - (col - low_col)) <= reach_col.astype(jnp.float32)
            )
            for row in range(classes):
                row_ok = jnp.abs(key_row - row) <= reach_row.astype(jnp.float32)
                shift = jnp.where(col_ok & row_ok, 0.0, MASKED)
                low = (col - start) * strip + row * half
                masked = scores[low : low + half, :] + shift
                top = jnp.max(masked, axis=1, keepdims=True)
                weights.append(jnp.exp2((masked - top) * scale))
        weights = jnp.concatenate(weights, 0).astype(jnp.bfloat16)
        sums = jnp.dot(weights, vs_ref[key_rows, :], preferred_element_type=jnp.float32)
        result = sums[:, :HEAD_DIM] / sums[:, HEAD_DIM:]
        for col in range(start, start + block_cols):
            for row in range(rows):
                low = row * FRAME_W + col * TILE_W
                got = (col - start) * strip + row * TILE_W
                lin_out_ref[low : low + TILE_W, :] = result[got : got + TILE_W, :]
    tokens = slots * chunk
    lin_out_ref[tokens:, :] = jnp.zeros(
        (lin_out_ref.shape[0] - tokens, HEAD_DIM), jnp.float32
    )
    for slot in range(slots):
        low = slot * chunk
        out_ref[slot] = lin_out_ref[low : low + slot_rows, :].astype(jnp.bfloat16)


def attend(meta, q, kv, before, after, chunk):
    slots, slot_rows, width = q.shape
    heads = width // HEAD_DIM
    tokens = slots * chunk
    lin_rows = padded(tokens + slot_rows - chunk)
    block = (slots, slot_rows, HEAD_DIM)
    own = pl.BlockSpec(block, lambda h: (0, 0, h))
    second = pl.BlockSpec(block, lambda h: (0, 0, h + heads))
    return pl.pallas_call(
        functools.partial(attend_kernel, chunk=chunk, block_cols=2, reach=2),
        out_shape=jax.ShapeDtypeStruct(q.shape, jnp.bfloat16),
        grid=(heads,),
        in_specs=[pl.BlockSpec(memory_space=pltpu.SMEM), own] + [own] * 3 + [second] * 3,
        out_specs=own,
        scratch_shapes=[
            pltpu.VMEM((lin_rows, HEAD_DIM), jnp.float32),
            pltpu.VMEM((tokens, HEAD_DIM), jnp.bfloat16),
            pltpu.VMEM((3 * tokens, HEAD_DIM), jnp.bfloat16),
            pltpu.VMEM((3 * tokens, 2 * HEAD_DIM), jnp.bfloat16),
            pltpu.VMEM((lin_rows, HEAD_DIM), jnp.float32),
        ],
        compiler_params=pltpu.CompilerParams(vmem_limit_bytes=32 * 2**20),
    )(meta, q, before, kv, after, before, kv, after)


def neighbours(slabs, groups, step):
    turned = [groups // 2 if slab >= slabs // 2 else 0 for slab in range(slabs)]
    pairs = []
    for slab in range(slabs):
        other = slab + step
        if 0 <= other < slabs:
            for group in range(groups):
                pairs.append(
                    (
                        slab * groups + (group ^ turned[slab]),
                        other * groups + (group ^ turned[other]),
                    )
                )
    return pairs


def swap(slots):
    return lax.all_to_all(slots, "head", split_axis=0, concat_axis=0)


def per_device(q_vals, k_vals, v_vals, q_scale, k_scale, v_scale, window):
    groups = lax.axis_size("head")
    slabs = lax.axis_size("slab")
    chunk = q_vals.shape[0]
    local_heads = q_scale.shape[1] // groups
    slab = lax.axis_index("slab")
    flip = jnp.where(slab >= slabs // 2, groups // 2, 0).astype(jnp.int32)
    group = lax.axis_index("head") ^ flip
    reach = lax.dynamic_slice_in_dim(window, group * local_heads, local_heads, 0)
    ends = jnp.stack([jnp.where(slab > 0, 0, 1), jnp.where(slab < slabs - 1, 2, 1)])
    meta = jnp.concatenate([reach.reshape(-1), ends.astype(jnp.int32)])
    flip = flip.reshape(1)
    both = ("slab", "head")
    kv = swap(pack(flip, [(k_vals, k_scale), (v_vals, v_scale)], groups))
    before = lax.ppermute(kv, both, neighbours(slabs, groups, 1))
    after = lax.ppermute(kv, both, neighbours(slabs, groups, -1))
    q = swap(pack(flip, [(q_vals, q_scale)], groups))
    attended = attend(meta, q, kv, before, after, chunk)
    return unpack(flip, swap(attended), chunk)


def solution(mesh):
    tokens = P(("slab", "head"), None)
    return jax.shard_map(
        per_device,
        mesh=mesh,
        in_specs=(tokens,) * 6 + (P(),),
        out_specs=tokens,
        check_vma=False,
    )
```

```python
import functools

import jax
import jax.numpy as jnp
from jax import lax
from jax.experimental import pallas as pl
from jax.experimental.pallas import tpu as pltpu
from jax.sharding import PartitionSpec as P

TILE_H = 5
TILE_W = 8
FRAME_W = 80
HEAD_DIM = 128
MASKED = -1e30
BLOCK_COLS = 2
MOST_COLS = 2
SCALE = 1.4426950408889634 / HEAD_DIM**0.5
VMEM_LIMIT = 32 * 2**20


def geometry(tokens):
    rows = tokens // FRAME_W
    return rows, FRAME_W // TILE_W, rows * TILE_W


def padded(rows):
    return -(-rows // 8) * 8


def params():
    return pltpu.CompilerParams(vmem_limit_bytes=VMEM_LIMIT)


def in_smem():
    return pl.BlockSpec(memory_space=pltpu.SMEM)


def in_vmem():
    return pl.BlockSpec(memory_space=pltpu.VMEM)


def pack_kernel(
    flip_ref, k_ref, v_ref, q_ref, ks_ref, vs_ref, qs_ref, kv_out, q_out, buf, scale_buf, sems
):
    groups, slot_rows, width = q_out.shape
    rows = k_ref.shape[0]
    heads = width // HEAD_DIM
    places = ((kv_out, 0), (kv_out, width), (q_out, 0))
    copies = [
        pltpu.make_async_copy(source, scale_buf.at[at], sems.at[at])
        for at, source in enumerate((ks_ref, vs_ref, qs_ref))
    ] + [
        pltpu.make_async_copy(source, buf.at[at], sems.at[len(places) + at])
        for at, source in enumerate((k_ref, v_ref, q_ref))
    ]
    for copy in copies:
        copy.start()
    for copy in copies:
        copy.wait()
    blank = jnp.zeros((slot_rows - rows, HEAD_DIM), jnp.float32)
    for at, (out_ref, low) in enumerate(places):
        scales = scale_buf[at].astype(jnp.float32).T
        for group in range(groups):
            for head in range(heads):
                index = group * heads + head
                vals = buf[at, :, index * HEAD_DIM : (index + 1) * HEAD_DIM]
                wide = vals.astype(jnp.float32) * scales[:, index : index + 1]
                if slot_rows > rows:
                    wide = jnp.concatenate([wide, blank], 0)
                start = low + head * HEAD_DIM
                out_ref[group ^ flip_ref[0], :, start : start + HEAD_DIM] = wide.astype(
                    jnp.bfloat16
                )


def pack(flip, k_vals, v_vals, q_vals, k_scale, v_scale, q_scale):
    groups = lax.axis_size("head")
    rows, full = k_vals.shape
    width = full // groups
    slot_rows = padded(rows)
    operands = [
        pltpu.with_memory_space_constraint(x, pltpu.HBM)
        for x in (k_vals, v_vals, q_vals, k_scale.T, v_scale.T, q_scale.T)
    ]
    return pl.pallas_call(
        pack_kernel,
        out_shape=(
            jax.ShapeDtypeStruct((groups, slot_rows, 2 * width), jnp.bfloat16),
            jax.ShapeDtypeStruct((groups, slot_rows, width), jnp.bfloat16),
        ),
        in_specs=[in_smem()] + [pl.BlockSpec(memory_space=pltpu.HBM)] * 6,
        out_specs=(in_vmem(), in_vmem()),
        scratch_shapes=[
            pltpu.VMEM((3, rows, full), jnp.bfloat16),
            pltpu.VMEM((3, k_scale.shape[1], rows), jnp.bfloat16),
            pltpu.SemaphoreType.DMA((6,)),
        ],
        compiler_params=params(),
    )(flip, *operands)


def unpack_kernel(flip_ref, in_ref, out_ref):
    groups, _, width = in_ref.shape
    rows = out_ref.shape[0]
    for group in range(groups):
        slot = in_ref[group ^ flip_ref[0]]
        out_ref[:, group * width : (group + 1) * width] = slot[:rows]


def unpack(flip, slots, rows):
    groups, _, width = slots.shape
    return pl.pallas_call(
        unpack_kernel,
        out_shape=jax.ShapeDtypeStruct((rows, groups * width), jnp.bfloat16),
        in_specs=[in_smem(), in_vmem()],
        out_specs=in_vmem(),
        compiler_params=params(),
    )(flip, slots)


def by_columns(slots_ref, lanes, lin_ref, chunk):
    slots = slots_ref.shape[0]
    rows, cols, _ = geometry(slots * chunk)
    for slot in range(slots):
        part = slots_ref[slot, :, lanes].astype(jnp.float32)
        lin_ref[slot * chunk : slot * chunk + part.shape[0], :] = part
    for col in range(cols):
        pieces = []
        for row in range(rows):
            low = row * FRAME_W + col * TILE_W
            pieces.append(lin_ref[low : low + TILE_W, :])
        yield col, jnp.concatenate(pieces, 0)


def blocks(cols, strip, span):
    found = []
    for start in range(0, cols, BLOCK_COLS):
        low = max(0, start - MOST_COLS)
        high = min(cols, start + BLOCK_COLS + MOST_COLS)
        query = slice(start * strip, (start + BLOCK_COLS) * strip)
        key = slice(low * span * strip, high * span * strip)
        found.append((start, low, query, key))
    return found


def shifts(block, strip, rows, frames, frame_reach, row_reach, col_reach):
    start, low_col, _, key = block
    span = len(frames)
    half = strip * TILE_H // rows
    at = lax.broadcasted_iota(jnp.int32, (1, key.stop - key.start), 1).astype(jnp.float32)
    key_col = jnp.floor((at + 0.5) * (1.0 / (span * strip)))
    rest = at - key_col * (span * strip)
    key_frame = jnp.floor((rest + 0.5) * (1.0 / strip))
    rest = rest - key_frame * strip
    key_row = jnp.floor((rest + 0.5) * (1.0 / half))
    gap = jnp.zeros_like(at)
    for frame, far in enumerate(frames):
        gap = jnp.where(key_frame == frame, far, gap)
    frame_ok = gap <= frame_reach
    for col in range(start, start + BLOCK_COLS):
        col_ok = frame_ok & (jnp.abs(key_col - (col - low_col)) <= col_reach)
        for row in range(rows // TILE_H):
            row_ok = jnp.abs(key_row - row) <= row_reach
            low = (col - start) * strip + row * half
            yield slice(low, low + half), jnp.where(col_ok & row_ok, 0.0, MASKED)


def attend_kernel(
    meta_ref, q_ref, own_ref, beside_ref, away_ref, out_ref, lin_ref, qs_ref, ks_ref, vs_ref,
    lin_out_ref, *, chunk,
):
    slots, slot_rows, width = out_ref.shape
    heads = width // HEAD_DIM
    tokens = slots * chunk
    rows, cols, strip = geometry(tokens)
    sources = (own_ref, beside_ref, away_ref)
    span = len(sources)
    vs_ref[:, HEAD_DIM:] = jnp.ones((vs_ref.shape[0], vs_ref.shape[1] - HEAD_DIM), vs_ref.dtype)
    lin_out_ref[tokens:, :] = jnp.zeros((lin_out_ref.shape[0] - tokens, HEAD_DIM), jnp.float32)
    away = jnp.where(meta_ref[3 * heads] > 0, 1.0, 2.0)

    @pl.loop(0, heads)
    def _(head):
        lanes = pl.ds(pl.multiple_of(head * HEAD_DIM, HEAD_DIM), HEAD_DIM)
        value_lanes = pl.ds(pl.multiple_of((heads + head) * HEAD_DIM, HEAD_DIM), HEAD_DIM)
        for col, part in by_columns(q_ref, lanes, lin_ref, chunk):
            qs_ref[col * strip : (col + 1) * strip, :] = part.astype(jnp.bfloat16)
        for frame, source in enumerate(sources):
            for take, target in ((lanes, ks_ref), (value_lanes, vs_ref)):
                for col, part in by_columns(source, take, lin_ref, chunk):
                    low = (col * span + frame) * strip
                    target[low : low + strip, :HEAD_DIM] = part.astype(jnp.bfloat16)
        reach = [meta_ref[3 * head + i].astype(jnp.float32) for i in range(3)]
        all_blocks = blocks(cols, strip, span)
        all_scores = [
            lax.dot_general(
                qs_ref[query, :],
                ks_ref[key, :],
                (((1,), (1,)), ((), ())),
                preferred_element_type=jnp.float32,
            )
            for _, _, query, key in all_blocks
        ]
        all_weights = []
        for block, scores in zip(all_blocks, all_scores):
            weights = []
            for mine, shift in shifts(block, strip, rows, (0.0, 1.0, away), *reach):
                masked = scores[mine, :] + shift
                top = jnp.max(masked, axis=1, keepdims=True)
                weights.append(jnp.exp2((masked - top) * SCALE))
            all_weights.append(jnp.concatenate(weights, 0).astype(jnp.bfloat16))
        for (start, _, _, key), weights in zip(all_blocks, all_weights):
            sums = jnp.dot(weights, vs_ref[key, :], preferred_element_type=jnp.float32)
            result = sums[:, :HEAD_DIM] / sums[:, HEAD_DIM:]
            for col in range(start, start + BLOCK_COLS):
                for row in range(rows):
                    low = row * FRAME_W + col * TILE_W
                    got = (col - start) * strip + row * TILE_W
                    lin_out_ref[low : low + TILE_W, :] = result[got : got + TILE_W, :]
        for slot in range(slots):
            low = slot * chunk
            out_ref[slot, :, lanes] = lin_out_ref[low : low + slot_rows, :].astype(jnp.bfloat16)


def attend(meta, q, own, beside, away, chunk):
    slots, slot_rows, width = q.shape
    tokens = slots * chunk
    lin_rows = padded(tokens + slot_rows - chunk)
    return pl.pallas_call(
        functools.partial(attend_kernel, chunk=chunk),
        out_shape=jax.ShapeDtypeStruct(q.shape, jnp.bfloat16),
        in_specs=[in_smem()] + [in_vmem()] * 4,
        out_specs=in_vmem(),
        scratch_shapes=[
            pltpu.VMEM((lin_rows, HEAD_DIM), jnp.float32),
            pltpu.VMEM((tokens, HEAD_DIM), jnp.bfloat16),
            pltpu.VMEM((3 * tokens, HEAD_DIM), jnp.bfloat16),
            pltpu.VMEM((3 * tokens, 2 * HEAD_DIM), jnp.bfloat16),
            pltpu.VMEM((lin_rows, HEAD_DIM), jnp.float32),
        ],
        compiler_params=params(),
    )(meta, q, own, beside, away)


def turn(slab, slabs, groups):
    return jnp.where(slab >= slabs // 2, groups // 2, 0)


def exchange(array, pairs):
    groups, slabs = lax.axis_size("head"), lax.axis_size("slab")
    turned = [0 if slab < slabs // 2 else groups // 2 for slab in range(slabs)]
    both = [
        (a * groups + (group ^ turned[a]), b * groups + (group ^ turned[b]))
        for low, high in pairs
        for a, b in ((low, high), (high, low))
        for group in range(groups)
    ]
    return lax.ppermute(array, ("slab", "head"), both)


def swap(slots):
    return lax.all_to_all(slots, "head", split_axis=0, concat_axis=0)


def per_device(q_vals, k_vals, v_vals, q_scale, k_scale, v_scale, window):
    groups = lax.axis_size("head")
    slabs = lax.axis_size("slab")
    chunk = q_vals.shape[0]
    local_heads = q_scale.shape[1] // groups
    slab = lax.axis_index("slab")
    flip = turn(slab, slabs, groups).astype(jnp.int32)
    low = (lax.axis_index("head") ^ flip) * local_heads
    flip = flip.reshape(1)
    reach = lax.dynamic_slice_in_dim(window, low, local_heads, 0)
    linked = ((slab > 0) & (slab < slabs - 1)).astype(jnp.int32)
    meta = jnp.concatenate([reach.reshape(-1), linked.reshape(1)])
    kv, q = pack(flip, k_vals, v_vals, q_vals, k_scale, v_scale, q_scale)
    kv = swap(kv)
    beside = exchange(kv, [(s, s + 1) for s in range(0, slabs, 2)])
    away = exchange(kv, [(s, s + 1) for s in range(1, slabs - 1, 2)])
    q = swap(q)
    attended = attend(meta, q, kv, beside, away, chunk)
    return unpack(flip, swap(attended), chunk)


def solution(mesh):
    tokens = P(("slab", "head"), None)
    return jax.shard_map(
        per_device,
        mesh=mesh,
        in_specs=(tokens,) * 6 + (P(),),
        out_specs=tokens,
        check_vma=False,
    )
```

```python
import functools

import jax
import jax.numpy as jnp
from jax import lax
from jax.experimental import pallas as pl
from jax.experimental.pallas import tpu as pltpu
from jax.sharding import PartitionSpec as P

TILE_H = 5
TILE_W = 8
FRAME_W = 80
HEAD_DIM = 128
MASKED = -1e30
BLOCK_COLS = 2
MOST_COLS = 2
SCALE = 1.4426950408889634 / HEAD_DIM**0.5
ORDER_FLOPS = 2 * 10**10


def geometry(tokens):
    rows = tokens // FRAME_W
    return rows, FRAME_W // TILE_W, rows * TILE_W


def padded(rows):
    return -(-rows // 8) * 8


def params(mib):
    return pltpu.CompilerParams(vmem_limit_bytes=mib * 2**20)


def in_smem():
    return pl.BlockSpec(memory_space=pltpu.SMEM)


def in_vmem():
    return pl.BlockSpec(memory_space=pltpu.VMEM)


def pack_kernel(
    flip_ref, k_ref, v_ref, q_ref, ks_ref, vs_ref, qs_ref, kv_out, q_out, buf, scale_buf, sems
):
    groups, slot_rows, width = q_out.shape
    rows = k_ref.shape[0]
    heads = width // HEAD_DIM
    copies = [
        pltpu.make_async_copy(source, scale_buf.at[at], sems.at[at])
        for at, source in enumerate((ks_ref, vs_ref, qs_ref))
    ] + [
        pltpu.make_async_copy(source, buf.at[at], sems.at[3 + at])
        for at, source in enumerate((k_ref, v_ref, q_ref))
    ]
    for copy in copies:
        copy.start()
    for copy in copies:
        copy.wait()
    blank = jnp.zeros((slot_rows - rows, HEAD_DIM), jnp.float32)
    scales = [scale_buf[at].astype(jnp.float32).T for at in range(3)]

    def scaled(at, index):
        vals = buf[at, :, index * HEAD_DIM : (index + 1) * HEAD_DIM]
        return vals.astype(jnp.float32) * scales[at][:, index : index + 1]

    for group in range(groups):
        indices = range(group * heads, (group + 1) * heads)
        stacked = [scaled(at, index) for index in indices for at in range(2)]
        slot = group ^ flip_ref[0]
        kv_out[slot] = jnp.concatenate(stacked, 0).astype(jnp.bfloat16)
    for group in range(groups):
        slot = group ^ flip_ref[0]
        for head in range(heads):
            wide = scaled(2, group * heads + head)
            if slot_rows > rows:
                wide = jnp.concatenate([wide, blank], 0)
            low = head * HEAD_DIM
            q_out[slot, :, low : low + HEAD_DIM] = wide.astype(jnp.bfloat16)


def pack(flip, k_vals, v_vals, q_vals, k_scale, v_scale, q_scale):
    groups = lax.axis_size("head")
    rows, full = k_vals.shape
    width = full // groups
    slot_rows = padded(rows)
    operands = [
        pltpu.with_memory_space_constraint(x, pltpu.HBM)
        for x in (k_vals, v_vals, q_vals, k_scale.T, v_scale.T, q_scale.T)
    ]
    return pl.pallas_call(
        pack_kernel,
        out_shape=(
            jax.ShapeDtypeStruct((groups, 2 * rows * (width // HEAD_DIM), HEAD_DIM), jnp.bfloat16),
            jax.ShapeDtypeStruct((groups, slot_rows, width), jnp.bfloat16),
        ),
        in_specs=[in_smem()] + [pl.BlockSpec(memory_space=pltpu.HBM)] * 6,
        out_specs=(in_vmem(), in_vmem()),
        scratch_shapes=[
            pltpu.VMEM((3, rows, full), jnp.bfloat16),
            pltpu.VMEM((3, k_scale.shape[1], rows), jnp.bfloat16),
            pltpu.SemaphoreType.DMA((6,)),
        ],
        compiler_params=params(8),
    )(flip, *operands)


def unpack_kernel(flip_ref, in_ref, out_ref):
    groups, _, width = in_ref.shape
    rows = out_ref.shape[0]
    for group in range(groups):
        slot = in_ref[group ^ flip_ref[0]]
        out_ref[:, group * width : (group + 1) * width] = slot[:rows]


def unpack(flip, slots, rows):
    groups, _, width = slots.shape
    return pl.pallas_call(
        unpack_kernel,
        out_shape=jax.ShapeDtypeStruct((rows, groups * width), jnp.bfloat16),
        in_specs=[in_smem(), in_vmem()],
        out_specs=in_vmem(),
        compiler_params=params(4),
    )(flip, slots)


def tokens_by_eight(slots, base, chunk):
    first_half = lax.broadcasted_iota(jnp.int32, (TILE_W, HEAD_DIM), 0) < TILE_W // 2
    half = TILE_W // 2
    turned = {}

    def aligned(slot, low):
        return slots[slot][low : low + TILE_W, :]

    def halves_swapped(slot, low):
        if (slot, low) not in turned:
            turned[slot, low] = pltpu.roll(aligned(slot, low), half, 0)
        return turned[slot, low]

    def upper(slot, low):
        return aligned(slot, low) if low % TILE_W == 0 else halves_swapped(slot, low - half)

    def lower(slot, low):
        return halves_swapped(slot, low) if low % TILE_W == 0 else aligned(slot, low - half)

    def eight(slot, low):
        if low % TILE_W == 0:
            return aligned(slot, low)
        return jnp.where(first_half, upper(slot, low), lower(slot, low + half))

    full = chunk // TILE_W
    for slot in range(0, len(slots), 2):
        for at in range(full):
            yield eight(slot, base + at * TILE_W)
        yield jnp.where(first_half, upper(slot, base + full * TILE_W), lower(slot + 1, base))
        for at in range(full):
            yield eight(slot + 1, base + half + at * TILE_W)


def by_columns(slots, base, chunk):
    cols = FRAME_W // TILE_W
    groups = list(tokens_by_eight(slots, base, chunk))
    return [jnp.concatenate(groups[col::cols], 0) for col in range(cols)]


def blocks(cols, strip, span):
    found = []
    for start in range(0, cols, BLOCK_COLS):
        low = max(0, start - MOST_COLS)
        high = min(cols, start + BLOCK_COLS + MOST_COLS)
        query = slice(start * strip, (start + BLOCK_COLS) * strip)
        key = slice(low * span * strip, high * span * strip)
        found.append((start, low, query, key))
    return found


def shifts(block, strip, rows, frames, frame_reach, row_reach, col_reach):
    start, low_col, _, key = block
    span = len(frames)
    half = strip * TILE_H // rows
    at = lax.broadcasted_iota(jnp.int32, (1, key.stop - key.start), 1).astype(jnp.float32)
    key_col = jnp.floor((at + 0.5) * (1.0 / (span * strip)))
    rest = at - key_col * (span * strip)
    key_frame = jnp.floor((rest + 0.5) * (1.0 / strip))
    rest = rest - key_frame * strip
    key_row = jnp.floor((rest + 0.5) * (1.0 / half))
    gap = jnp.zeros_like(at)
    for frame, far in enumerate(frames):
        gap = jnp.where(key_frame == frame, far, gap)
    frame_ok = gap <= frame_reach
    for col in range(start, start + BLOCK_COLS):
        col_ok = frame_ok & (jnp.abs(key_col - (col - low_col)) <= col_reach)
        for row in range(rows // TILE_H):
            row_ok = jnp.abs(key_row - row) <= row_reach
            low = (col - start) * strip + row * half
            yield slice(low, low + half), jnp.where(col_ok & row_ok, 0.0, MASKED)


def attend_kernel(
    meta_ref, q_ref, own_ref, beside_ref, away_ref, out_ref, qs_ref, ks_ref, vs_ref, lin_out_ref, *, chunk,
):
    slots, slot_rows, width = out_ref.shape
    heads = width // HEAD_DIM
    tokens = slots * chunk
    rows, cols, strip = geometry(tokens)
    sources = (own_ref, beside_ref, away_ref)
    span = len(sources)
    ones = jnp.ones((vs_ref.shape[1], vs_ref.shape[2] - HEAD_DIM), vs_ref.dtype)
    for head in range(heads):
        vs_ref[head, :, HEAD_DIM:] = ones
    lin_out_ref[tokens:, :] = jnp.zeros((lin_out_ref.shape[0] - tokens, HEAD_DIM), jnp.float32)
    away = jnp.where(meta_ref[3 * heads] > 0, 1.0, 2.0)

    for frame, source in enumerate(sources):
        taken = [source[slot].astype(jnp.float32) for slot in range(slots)]
        for head in range(heads):
            for at, target in enumerate((ks_ref, vs_ref)):
                for col, part in enumerate(by_columns(taken, (2 * head + at) * chunk, chunk)):
                    low = (col * span + frame) * strip
                    target[head, low : low + strip, :HEAD_DIM] = part.astype(jnp.bfloat16)
    for head in range(heads):
        lanes = slice(head * HEAD_DIM, (head + 1) * HEAD_DIM)
        taken = [q_ref[slot, :, lanes].astype(jnp.float32) for slot in range(slots)]
        for col, part in enumerate(by_columns(taken, 0, chunk)):
            qs_ref[head, col * strip : (col + 1) * strip, :] = part.astype(jnp.bfloat16)

    @pl.loop(0, heads)
    def _(head):
        lanes = pl.ds(pl.multiple_of(head * HEAD_DIM, HEAD_DIM), HEAD_DIM)
        reach = [meta_ref[3 * head + i].astype(jnp.float32) for i in range(3)]
        all_blocks = blocks(cols, strip, span)
        all_scores = [
            lax.dot_general(
                qs_ref[head, query, :],
                ks_ref[head, key, :],
                (((1,), (1,)), ((), ())),
                preferred_element_type=jnp.float32,
            )
            for _, _, query, key in all_blocks
        ]
        all_weights = []
        for block, scores in zip(all_blocks, all_scores):
            weights = []
            for mine, shift in shifts(block, strip, rows, (0.0, 1.0, away), *reach):
                masked = scores[mine, :] + shift
                top = jnp.max(masked, axis=1, keepdims=True)
                weights.append(jnp.exp2((masked - top) * SCALE))
            all_weights.append(jnp.concatenate(weights, 0).astype(jnp.bfloat16))
        for (start, _, _, key), weights in zip(all_blocks, all_weights):
            sums = jnp.dot(weights, vs_ref[head, key, :], preferred_element_type=jnp.float32)
            result = sums[:, :HEAD_DIM] / sums[:, HEAD_DIM:]
            for col in range(start, start + BLOCK_COLS):
                for row in range(rows):
                    low = row * FRAME_W + col * TILE_W
                    got = (col - start) * strip + row * TILE_W
                    lin_out_ref[low : low + TILE_W, :] = result[got : got + TILE_W, :]
        for slot in range(slots):
            low = slot * chunk
            out_ref[slot, :, lanes] = lin_out_ref[low : low + slot_rows, :].astype(jnp.bfloat16)


def attend(meta, q, own, beside, away, chunk):
    slots, slot_rows, width = q.shape
    heads = width // HEAD_DIM
    tokens = slots * chunk
    lin_rows = padded(tokens + slot_rows - chunk)
    return pl.pallas_call(
        functools.partial(attend_kernel, chunk=chunk),
        out_shape=jax.ShapeDtypeStruct(q.shape, jnp.bfloat16),
        in_specs=[in_smem()] + [in_vmem()] * 4,
        out_specs=in_vmem(),
        scratch_shapes=[
            pltpu.VMEM((heads, tokens, HEAD_DIM), jnp.bfloat16),
            pltpu.VMEM((heads, 3 * tokens, HEAD_DIM), jnp.bfloat16),
            pltpu.VMEM((heads, 3 * tokens, 2 * HEAD_DIM), jnp.bfloat16),
            pltpu.VMEM((lin_rows, HEAD_DIM), jnp.float32),
        ],
        compiler_params=params(16),
    )(meta, q, own, beside, away)


def after_kernel(meta_ref, array_ref, out_ref):
    for at in range(meta_ref.shape[0]):
        out_ref[at] = meta_ref[at]


def after(meta, array):
    return pl.pallas_call(
        after_kernel,
        out_shape=jax.ShapeDtypeStruct(meta.shape, meta.dtype),
        in_specs=[in_smem(), pl.BlockSpec(memory_space=pl.ANY)],
        out_specs=in_smem(),
        compiler_params=params(1),
        cost_estimate=pl.CostEstimate(flops=ORDER_FLOPS, bytes_accessed=0, transcendentals=0),
    )(meta, array)


def turn(slab, slabs, groups):
    return jnp.where(slab >= slabs // 2, groups // 2, 0)


def exchange(array, pairs):
    groups, slabs = lax.axis_size("head"), lax.axis_size("slab")
    turned = [0 if slab < slabs // 2 else groups // 2 for slab in range(slabs)]
    both = [
        (a * groups + (group ^ turned[a]), b * groups + (group ^ turned[b]))
        for low, high in pairs
        for a, b in ((low, high), (high, low))
        for group in range(groups)
    ]
    return lax.ppermute(array, ("slab", "head"), both)


def swap(slots):
    return lax.all_to_all(slots, "head", split_axis=0, concat_axis=0)


def per_device(q_vals, k_vals, v_vals, q_scale, k_scale, v_scale, window):
    groups = lax.axis_size("head")
    slabs = lax.axis_size("slab")
    chunk = q_vals.shape[0]
    local_heads = q_scale.shape[1] // groups
    slab = lax.axis_index("slab")
    flip = turn(slab, slabs, groups).astype(jnp.int32)
    low = (lax.axis_index("head") ^ flip) * local_heads
    flip = flip.reshape(1)
    reach = lax.dynamic_slice_in_dim(window, low, local_heads, 0)
    linked = ((slab > 0) & (slab < slabs - 1)).astype(jnp.int32)
    meta = jnp.concatenate([reach.reshape(-1), linked.reshape(1)])
    kv, q = pack(flip, k_vals, v_vals, q_vals, k_scale, v_scale, q_scale)
    kv = swap(kv)
    away = exchange(kv, [(s, s + 1) for s in range(1, slabs - 1, 2)])
    beside = exchange(kv, [(s, s + 1) for s in range(0, slabs, 2)])
    q = swap(q)
    meta = after(meta, away)
    attended = attend(meta, q, kv, beside, away, chunk)
    return unpack(flip, swap(attended), chunk)


def solution(mesh):
    tokens = P(("slab", "head"), None)
    return jax.shard_map(
        per_device,
        mesh=mesh,
        in_specs=(tokens,) * 6 + (P(),),
        out_specs=tokens,
        check_vma=False,
    )
```

```python
import functools

import jax
import jax.numpy as jnp
from jax import lax
from jax.experimental import pallas as pl
from jax.experimental.pallas import tpu as pltpu
from jax.sharding import PartitionSpec as P

TILE_H = 5
TILE_W = 8
FRAME_W = 80
HEAD_DIM = 128
MASKED = -1e30
BLOCK_COLS = 2
MOST_COLS = 2
SCALE = 1.4426950408889634 / HEAD_DIM**0.5
ORDER_FLOPS = 2 * 10**10


def geometry(tokens):
    rows = tokens // FRAME_W
    return rows, FRAME_W // TILE_W, rows * TILE_W


def padded(rows):
    return -(-rows // 8) * 8


def params(mib):
    return pltpu.CompilerParams(vmem_limit_bytes=mib * 2**20)


def in_smem():
    return pl.BlockSpec(memory_space=pltpu.SMEM)


def in_vmem():
    return pl.BlockSpec(memory_space=pltpu.VMEM)


def pack_kernel(
    flip_ref, k_ref, v_ref, q_ref, ks_ref, vs_ref, qs_ref, kv_out, q_out, buf, scale_buf, sems
):
    groups, slot_rows, width = q_out.shape
    rows = k_ref.shape[0]
    heads = width // HEAD_DIM
    copies = [
        pltpu.make_async_copy(source, scale_buf.at[at], sems.at[at])
        for at, source in enumerate((ks_ref, vs_ref, qs_ref))
    ] + [
        pltpu.make_async_copy(source, buf.at[at], sems.at[3 + at])
        for at, source in enumerate((k_ref, v_ref, q_ref))
    ]
    for copy in copies:
        copy.start()
    for copy in copies:
        copy.wait()
    blank = jnp.zeros((slot_rows - rows, HEAD_DIM), jnp.float32)
    scales = [scale_buf[at].astype(jnp.float32).T for at in range(3)]

    def scaled(at, index):
        vals = buf[at, :, index * HEAD_DIM : (index + 1) * HEAD_DIM]
        return vals.astype(jnp.float32) * scales[at][:, index : index + 1]

    for group in range(groups):
        indices = range(group * heads, (group + 1) * heads)
        stacked = [scaled(at, index) for index in indices for at in range(2)]
        slot = group ^ flip_ref[0]
        kv_out[slot] = jnp.concatenate(stacked, 0).astype(jnp.bfloat16)
    for group in range(groups):
        slot = group ^ flip_ref[0]
        for head in range(heads):
            wide = scaled(2, group * heads + head)
            if slot_rows > rows:
                wide = jnp.concatenate([wide, blank], 0)
            low = head * HEAD_DIM
            q_out[slot, :, low : low + HEAD_DIM] = wide.astype(jnp.bfloat16)


def pack(flip, k_vals, v_vals, q_vals, k_scale, v_scale, q_scale):
    groups = lax.axis_size("head")
    rows, full = k_vals.shape
    width = full // groups
    slot_rows = padded(rows)
    operands = [
        pltpu.with_memory_space_constraint(x, pltpu.HBM)
        for x in (k_vals, v_vals, q_vals, k_scale.T, v_scale.T, q_scale.T)
    ]
    return pl.pallas_call(
        pack_kernel,
        out_shape=(
            jax.ShapeDtypeStruct((groups, 2 * rows * (width // HEAD_DIM), HEAD_DIM), jnp.bfloat16),
            jax.ShapeDtypeStruct((groups, slot_rows, width), jnp.bfloat16),
        ),
        in_specs=[in_smem()] + [pl.BlockSpec(memory_space=pltpu.HBM)] * 6,
        out_specs=(in_vmem(), in_vmem()),
        scratch_shapes=[
            pltpu.VMEM((3, rows, full), jnp.bfloat16),
            pltpu.VMEM((3, k_scale.shape[1], rows), jnp.bfloat16),
            pltpu.SemaphoreType.DMA((6,)),
        ],
        compiler_params=params(8),
    )(flip, *operands)


def unpack_kernel(flip_ref, in_ref, out_ref):
    groups, _, width = in_ref.shape
    rows = out_ref.shape[0]
    for group in range(groups):
        slot = in_ref[group ^ flip_ref[0]]
        out_ref[:, group * width : (group + 1) * width] = slot[:rows]


def unpack(flip, slots, rows):
    groups, _, width = slots.shape
    return pl.pallas_call(
        unpack_kernel,
        out_shape=jax.ShapeDtypeStruct((rows, groups * width), jnp.bfloat16),
        in_specs=[in_smem(), in_vmem()],
        out_specs=in_vmem(),
        compiler_params=params(4),
    )(flip, slots)


def tokens_by_eight(slots, base, chunk):
    first_half = lax.broadcasted_iota(jnp.int32, (TILE_W, HEAD_DIM), 0) < TILE_W // 2
    half = TILE_W // 2
    turned = {}

    def aligned(slot, low):
        return slots[slot][low : low + TILE_W, :]

    def halves_swapped(slot, low):
        if (slot, low) not in turned:
            turned[slot, low] = pltpu.roll(aligned(slot, low), half, 0)
        return turned[slot, low]

    def upper(slot, low):
        return aligned(slot, low) if low % TILE_W == 0 else halves_swapped(slot, low - half)

    def lower(slot, low):
        return halves_swapped(slot, low) if low % TILE_W == 0 else aligned(slot, low - half)

    def eight(slot, low):
        if low % TILE_W == 0:
            return aligned(slot, low)
        return jnp.where(first_half, upper(slot, low), lower(slot, low + half))

    full = chunk // TILE_W
    for slot in range(0, len(slots), 2):
        for at in range(full):
            yield eight(slot, base + at * TILE_W)
        yield jnp.where(first_half, upper(slot, base + full * TILE_W), lower(slot + 1, base))
        for at in range(full):
            yield eight(slot + 1, base + half + at * TILE_W)


def by_columns(slots, base, chunk):
    cols = FRAME_W // TILE_W
    groups = list(tokens_by_eight(slots, base, chunk))
    return [jnp.concatenate(groups[col::cols], 0) for col in range(cols)]


def blocks(cols, reach):
    for start in range(0, cols, BLOCK_COLS):
        yield start, max(0, start - reach), min(cols, start + BLOCK_COLS + reach)


def shifts(block, strip, rows, frames, frame_reach, row_reach, col_reach):
    start, low_col, high_col = block
    span = len(frames)
    half = strip * TILE_H // rows
    keys = (high_col - low_col) * span * strip
    at = lax.broadcasted_iota(jnp.int32, (1, keys), 1).astype(jnp.float32)
    key_col = jnp.floor((at + 0.5) * (1.0 / (span * strip)))
    rest = at - key_col * (span * strip)
    key_frame = jnp.floor((rest + 0.5) * (1.0 / strip))
    rest = rest - key_frame * strip
    key_row = jnp.floor((rest + 0.5) * (1.0 / half))
    gap = jnp.zeros_like(at)
    for frame, far in enumerate(frames):
        gap = jnp.where(key_frame == frame, far, gap)
    frame_ok = gap <= frame_reach
    for col in range(start, start + BLOCK_COLS):
        col_ok = frame_ok & (jnp.abs(key_col - (col - low_col)) <= col_reach)
        for row in range(rows // TILE_H):
            row_ok = jnp.abs(key_row - row) <= row_reach
            low = (col - start) * strip + row * half
            yield slice(low, low + half), jnp.where(col_ok & row_ok, 0.0, MASKED)


def attend_kernel(
    zeros_ref, meta_ref, q_ref, own_ref, away_ref, beside_hbm, out_ref, qs_ref, ks_ref, vs_ref, lin_out_ref,
    beside_ref, sem, *, chunk,
):
    slots, slot_rows, width = out_ref.shape
    heads = width // HEAD_DIM
    tokens = slots * chunk
    rows, cols, strip = geometry(tokens)
    span = 3
    copy = pltpu.make_async_copy(beside_hbm, beside_ref, sem)
    copy.start()
    ones = jnp.ones((vs_ref.shape[1], vs_ref.shape[2] - HEAD_DIM), vs_ref.dtype)
    for head in range(heads):
        vs_ref[head, :, HEAD_DIM:] = ones
    lin_out_ref[tokens:, :] = zeros_ref[: lin_out_ref.shape[0] - tokens, :]
    away = jnp.where(meta_ref[3 * heads] > 0, 1.0, 2.0)

    for head in range(heads):
        lanes = slice(head * HEAD_DIM, (head + 1) * HEAD_DIM)
        taken = [q_ref[slot, :, lanes].astype(jnp.float32) for slot in range(slots)]
        for col, part in enumerate(by_columns(taken, 0, chunk)):
            qs_ref[head, col * strip : (col + 1) * strip, :] = part.astype(jnp.bfloat16)

    def by_head(frame, source, head):
        taken = [source[slot].astype(jnp.float32) for slot in range(slots)]
        for at, target in enumerate((ks_ref, vs_ref)):
            for col, part in enumerate(by_columns(taken, (2 * head + at) * chunk, chunk)):
                low = (col * span + frame) * strip
                target[head, low : low + strip, :HEAD_DIM] = part.astype(jnp.bfloat16)

    for head in range(heads):
        by_head(0, own_ref, head)
    copy.wait()
    for head in range(heads):

        @pl.when(meta_ref[3 * head] > 0)
        def _(head=head):
            by_head(1, beside_ref, head)
            by_head(2, away_ref, head)

    def columns(ref, head, low, high, frames):
        if len(frames) == span:
            return ref[head, low * span * strip : high * span * strip, :]
        first = [col * span * strip for col in range(low, high)]
        return jnp.concatenate([ref[head, at : at + strip, :] for at in first], 0)

    def one_head(head, frames, most_cols):
        reach = [meta_ref[3 * head + i].astype(jnp.float32) for i in range(3)]
        all_blocks = list(blocks(cols, most_cols))
        all_scores = [
            lax.dot_general(
                qs_ref[head, start * strip : (start + BLOCK_COLS) * strip, :],
                columns(ks_ref, head, low, high, frames),
                (((1,), (1,)), ((), ())),
                preferred_element_type=jnp.float32,
            )
            for start, low, high in all_blocks
        ]
        all_weights = []
        for block, scores in zip(all_blocks, all_scores):
            weights = []
            for mine, shift in shifts(block, strip, rows, frames, *reach):
                masked = scores[mine, :] + shift
                top = jnp.max(masked, axis=1, keepdims=True)
                weights.append(jnp.exp2((masked - top) * SCALE))
            all_weights.append(jnp.concatenate(weights, 0).astype(jnp.bfloat16))
        for (start, low, high), weights in zip(all_blocks, all_weights):
            values = columns(vs_ref, head, low, high, frames)
            sums = jnp.dot(weights, values, preferred_element_type=jnp.float32)
            result = sums[:, :HEAD_DIM] / sums[:, HEAD_DIM:]
            for col in range(start, start + BLOCK_COLS):
                for row in range(rows):
                    low_row = row * FRAME_W + col * TILE_W
                    got = (col - start) * strip + row * TILE_W
                    lin_out_ref[low_row : low_row + TILE_W, :] = result[got : got + TILE_W, :]

    @pl.loop(0, heads)
    def _(head):
        more_frames = meta_ref[3 * head] > 0
        most = meta_ref[3 * head + 2] >= MOST_COLS

        @pl.when(more_frames & most)
        def _():
            one_head(head, (0.0, 1.0, away), MOST_COLS)

        @pl.when(more_frames & jnp.logical_not(most))
        def _():
            one_head(head, (0.0, 1.0, away), MOST_COLS - 1)

        @pl.when(jnp.logical_not(more_frames))
        def _():
            one_head(head, (0.0,), MOST_COLS)

        lanes = pl.ds(pl.multiple_of(head * HEAD_DIM, HEAD_DIM), HEAD_DIM)
        for slot in range(slots):
            low = slot * chunk
            out_ref[slot, :, lanes] = lin_out_ref[low : low + slot_rows, :].astype(jnp.bfloat16)


def attend(zeros, meta, q, own, beside, away, chunk):
    slots, slot_rows, width = q.shape
    heads = width // HEAD_DIM
    tokens = slots * chunk
    lin_rows = padded(tokens + slot_rows - chunk)
    hbm = pl.BlockSpec(memory_space=pltpu.HBM)
    return pl.pallas_call(
        functools.partial(attend_kernel, chunk=chunk),
        out_shape=jax.ShapeDtypeStruct(q.shape, jnp.bfloat16),
        in_specs=[in_vmem(), in_smem()] + [in_vmem()] * 3 + [hbm],
        out_specs=in_vmem(),
        scratch_shapes=[
            pltpu.VMEM((heads, tokens, HEAD_DIM), jnp.bfloat16),
            pltpu.VMEM((heads, 3 * tokens, HEAD_DIM), jnp.bfloat16),
            pltpu.VMEM((heads, 3 * tokens, 2 * HEAD_DIM), jnp.bfloat16),
            pltpu.VMEM((lin_rows, HEAD_DIM), jnp.float32),
            pltpu.VMEM(beside.shape, beside.dtype),
            pltpu.SemaphoreType.DMA,
        ],
        compiler_params=params(16),
    )(zeros, meta, q, own, away, pltpu.with_memory_space_constraint(beside, pltpu.HBM))


def after_kernel(array_ref, out_ref):
    out_ref[...] = jnp.zeros_like(out_ref)


def after(array):
    return pl.pallas_call(
        after_kernel,
        out_shape=jax.ShapeDtypeStruct((8, HEAD_DIM), jnp.float32),
        in_specs=[pl.BlockSpec(memory_space=pl.ANY)],
        out_specs=in_vmem(),
        compiler_params=params(1),
        cost_estimate=pl.CostEstimate(flops=ORDER_FLOPS, bytes_accessed=0, transcendentals=0),
    )(array)


def turn(slab, slabs, groups):
    return jnp.where(slab >= slabs // 2, groups // 2, 0)


def exchange(array, pairs):
    groups, slabs = lax.axis_size("head"), lax.axis_size("slab")
    turned = [0 if slab < slabs // 2 else groups // 2 for slab in range(slabs)]
    both = [
        (a * groups + (group ^ turned[a]), b * groups + (group ^ turned[b]))
        for low, high in pairs
        for a, b in ((low, high), (high, low))
        for group in range(groups)
    ]
    return lax.ppermute(array, ("slab", "head"), both)


def swap(slots):
    return lax.all_to_all(slots, "head", split_axis=0, concat_axis=0)


def per_device(q_vals, k_vals, v_vals, q_scale, k_scale, v_scale, window):
    groups = lax.axis_size("head")
    slabs = lax.axis_size("slab")
    chunk = q_vals.shape[0]
    local_heads = q_scale.shape[1] // groups
    slab = lax.axis_index("slab")
    flip = turn(slab, slabs, groups).astype(jnp.int32)
    low = (lax.axis_index("head") ^ flip) * local_heads
    flip = flip.reshape(1)
    reach = lax.dynamic_slice_in_dim(window, low, local_heads, 0)
    linked = ((slab > 0) & (slab < slabs - 1)).astype(jnp.int32)
    meta = jnp.concatenate([reach.reshape(-1), linked.reshape(1)])
    kv, q = pack(flip, k_vals, v_vals, q_vals, k_scale, v_scale, q_scale)
    kv = swap(kv)
    away = exchange(kv, [(s, s + 1) for s in range(1, slabs - 1, 2)])
    beside = exchange(kv, [(s, s + 1) for s in range(0, slabs, 2)])
    q = swap(q)
    attended = attend(after(away), meta, q, kv, beside, away, chunk)
    return unpack(flip, swap(attended), chunk)


def solution(mesh):
    tokens = P(("slab", "head"), None)
    return jax.shard_map(
        per_device,
        mesh=mesh,
        in_specs=(tokens,) * 6 + (P(),),
        out_specs=tokens,
        check_vma=False,
    )
```

```python
import functools

import jax
import jax.numpy as jnp
from jax import lax
from jax.experimental import pallas as pl
from jax.experimental.pallas import tpu as pltpu
from jax.sharding import PartitionSpec as P

TILE_H = 5
TILE_W = 8
FRAME_W = 80
HEAD_DIM = 128
MASKED = -1e30
BLOCK_COLS = 2
MOST_COLS = 2
SCALE = 1.4426950408889634 / HEAD_DIM**0.5
ORDER_FLOPS = 2 * 10**10


def geometry(tokens):
    rows = tokens // FRAME_W
    return rows, FRAME_W // TILE_W, rows * TILE_W


def padded(rows):
    return -(-rows // 8) * 8


def params(mib):
    return pltpu.CompilerParams(vmem_limit_bytes=mib * 2**20)


def in_smem():
    return pl.BlockSpec(memory_space=pltpu.SMEM)


def in_vmem():
    return pl.BlockSpec(memory_space=pltpu.VMEM)


def pack_kernel(
    flip_ref, k_ref, v_ref, q_ref, ks_ref, vs_ref, qs_ref, kv_out, q_out, buf, scale_buf, sems
):
    groups, slot_rows, width = q_out.shape
    rows = k_ref.shape[0]
    heads = width // HEAD_DIM
    copies = [
        pltpu.make_async_copy(source, scale_buf.at[at], sems.at[at])
        for at, source in enumerate((ks_ref, vs_ref, qs_ref))
    ]
    copies += [
        pltpu.make_async_copy(source, buf.at[at], sems.at[3 + at])
        for at, source in enumerate((k_ref, v_ref, q_ref))
    ]
    for copy in copies:
        copy.start()
    for copy in copies[:-1]:
        copy.wait()
    blank = jnp.zeros((slot_rows - rows, HEAD_DIM), jnp.float32)
    scales = [scale_buf[at].astype(jnp.float32).T for at in range(3)]

    def scaled(at, index):
        vals = buf[at, :, index * HEAD_DIM : (index + 1) * HEAD_DIM]
        return vals.astype(jnp.float32) * scales[at][:, index : index + 1]

    for group in range(groups):
        indices = range(group * heads, (group + 1) * heads)
        stacked = [scaled(at, index) for index in indices for at in range(2)]
        slot = group ^ flip_ref[0]
        kv_out[slot] = jnp.concatenate(stacked, 0).astype(jnp.bfloat16)
    copies[-1].wait()
    for group in range(groups):
        slot = group ^ flip_ref[0]
        for head in range(heads):
            wide = scaled(2, group * heads + head)
            if slot_rows > rows:
                wide = jnp.concatenate([wide, blank], 0)
            low = head * HEAD_DIM
            q_out[slot, :, low : low + HEAD_DIM] = wide.astype(jnp.bfloat16)


def pack(flip, k_vals, v_vals, q_vals, k_scale, v_scale, q_scale):
    groups = lax.axis_size("head")
    rows, full = k_vals.shape
    width = full // groups
    slot_rows = padded(rows)
    operands = [
        pltpu.with_memory_space_constraint(x, pltpu.HBM)
        for x in (k_vals, v_vals, q_vals, k_scale.T, v_scale.T, q_scale.T)
    ]
    return pl.pallas_call(
        pack_kernel,
        out_shape=(
            jax.ShapeDtypeStruct((groups, 2 * rows * (width // HEAD_DIM), HEAD_DIM), jnp.bfloat16),
            jax.ShapeDtypeStruct((groups, slot_rows, width), jnp.bfloat16),
        ),
        in_specs=[in_smem()] + [pl.BlockSpec(memory_space=pltpu.HBM)] * 6,
        out_specs=(in_vmem(), in_vmem()),
        scratch_shapes=[
            pltpu.VMEM((3, rows, full), jnp.bfloat16),
            pltpu.VMEM((3, k_scale.shape[1], rows), jnp.bfloat16),
            pltpu.SemaphoreType.DMA((6,)),
        ],
        compiler_params=params(8),
    )(flip, *operands)


def unpack_kernel(flip_ref, in_ref, out_ref):
    groups, _, width = in_ref.shape
    rows = out_ref.shape[0]
    for group in range(groups):
        slot = in_ref[group ^ flip_ref[0]]
        out_ref[:, group * width : (group + 1) * width] = slot[:rows]


def unpack(flip, slots, rows):
    groups, _, width = slots.shape
    return pl.pallas_call(
        unpack_kernel,
        out_shape=jax.ShapeDtypeStruct((rows, groups * width), jnp.bfloat16),
        in_specs=[in_smem(), in_vmem()],
        out_specs=in_vmem(),
        compiler_params=params(4),
    )(flip, slots)


def tokens_by_eight(slots, base, chunk):
    first_half = lax.broadcasted_iota(jnp.int32, (TILE_W, HEAD_DIM), 0) < TILE_W // 2
    half = TILE_W // 2
    turned = {}

    def aligned(slot, low):
        return slots[slot][low : low + TILE_W, :]

    def halves_swapped(slot, low):
        if (slot, low) not in turned:
            turned[slot, low] = pltpu.roll(aligned(slot, low), half, 0)
        return turned[slot, low]

    def upper(slot, low):
        return aligned(slot, low) if low % TILE_W == 0 else halves_swapped(slot, low - half)

    def lower(slot, low):
        return halves_swapped(slot, low) if low % TILE_W == 0 else aligned(slot, low - half)

    def eight(slot, low):
        if low % TILE_W == 0:
            return aligned(slot, low)
        return jnp.where(first_half, upper(slot, low), lower(slot, low + half))

    full = chunk // TILE_W
    for slot in range(0, len(slots), 2):
        for at in range(full):
            yield eight(slot, base + at * TILE_W)
        yield jnp.where(first_half, upper(slot, base + full * TILE_W), lower(slot + 1, base))
        for at in range(full):
            yield eight(slot + 1, base + half + at * TILE_W)


def by_columns(slots, base, chunk):
    cols = FRAME_W // TILE_W
    groups = list(tokens_by_eight(slots, base, chunk))
    return [jnp.concatenate(groups[col::cols], 0) for col in range(cols)]


def blocks(cols, reach):
    for start in range(0, cols, BLOCK_COLS):
        yield start, max(0, start - reach), min(cols, start + BLOCK_COLS + reach)


def shifts(block, strip, rows, frames, frame_reach, row_reach, col_reach):
    start, low_col, high_col = block
    span = len(frames)
    half = strip * TILE_H // rows
    keys = (high_col - low_col) * span * strip
    at = lax.broadcasted_iota(jnp.int32, (1, keys), 1).astype(jnp.float32)
    key_col = jnp.floor((at + 0.5) * (1.0 / (span * strip)))
    rest = at - key_col * (span * strip)
    key_frame = jnp.floor((rest + 0.5) * (1.0 / strip))
    rest = rest - key_frame * strip
    key_row = jnp.floor((rest + 0.5) * (1.0 / half))
    gap = jnp.zeros_like(at)
    for frame, far in enumerate(frames):
        gap = jnp.where(key_frame == frame, far, gap)
    frame_ok = gap <= frame_reach
    for col in range(start, start + BLOCK_COLS):
        col_ok = frame_ok & (jnp.abs(key_col - (col - low_col)) <= col_reach)
        for row in range(rows // TILE_H):
            row_ok = jnp.abs(key_row - row) <= row_reach
            low = (col - start) * strip + row * half
            yield slice(low, low + half), jnp.where(col_ok & row_ok, 0.0, MASKED)


def attend_kernel(
    zeros_ref, meta_ref, q_ref, own_ref, away_ref, beside_hbm, out_ref, qs_ref, ks_ref, vs_ref, lin_out_ref,
    beside_ref, sem, *, chunk,
):
    slots, slot_rows, width = out_ref.shape
    heads = width // HEAD_DIM
    tokens = slots * chunk
    rows, cols, strip = geometry(tokens)
    span = 3
    copy = pltpu.make_async_copy(beside_hbm, beside_ref, sem)
    copy.start()
    lin_out_ref[tokens:, :] = zeros_ref[: lin_out_ref.shape[0] - tokens, :]
    away = jnp.where(meta_ref[3 * heads] > 0, 1.0, 2.0)

    for head in range(heads):
        lanes = slice(head * HEAD_DIM, (head + 1) * HEAD_DIM)
        taken = [q_ref[slot, :, lanes].astype(jnp.float32) for slot in range(slots)]
        for col, part in enumerate(by_columns(taken, 0, chunk)):
            qs_ref[head, col * strip : (col + 1) * strip, :] = part.astype(jnp.bfloat16)

    def by_head(frame, source, head):
        taken = [source[slot].astype(jnp.float32) for slot in range(slots)]
        for at, target in enumerate((ks_ref, vs_ref)):
            for col, part in enumerate(by_columns(taken, (2 * head + at) * chunk, chunk)):
                low = (col * span + frame) * strip
                target[head, low : low + strip, :HEAD_DIM] = part.astype(jnp.bfloat16)

    for head in range(heads):
        by_head(0, own_ref, head)
    for frame, source in ((2, away_ref), (1, beside_ref)):
        if source is beside_ref:
            copy.wait()
        for head in range(heads):

            @pl.when(meta_ref[3 * head] > 0)
            def _(frame=frame, source=source, head=head):
                by_head(frame, source, head)

    def columns(ref, head, low, high, frames):
        if len(frames) == span:
            return ref[head, low * span * strip : high * span * strip, :]
        first = [col * span * strip for col in range(low, high)]
        return jnp.concatenate([ref[head, at : at + strip, :] for at in first], 0)

    def one_head(head, frames, most_cols):
        reach = [meta_ref[3 * head + i].astype(jnp.float32) for i in range(3)]
        all_blocks = list(blocks(cols, most_cols))
        all_scores = [
            lax.dot_general(
                qs_ref[head, start * strip : (start + BLOCK_COLS) * strip, :],
                columns(ks_ref, head, low, high, frames),
                (((1,), (1,)), ((), ())),
                preferred_element_type=jnp.float32,
            )
            for start, low, high in all_blocks
        ]
        all_weights = []
        for block, scores in zip(all_blocks, all_scores):
            weights = []
            for mine, shift in shifts(block, strip, rows, frames, *reach):
                masked = scores[mine, :] + shift
                top = jnp.max(masked, axis=1, keepdims=True)
                weights.append(jnp.exp2((masked - top) * SCALE))
            all_weights.append(jnp.concatenate(weights, 0).astype(jnp.bfloat16))
        for (start, low, high), weights in zip(all_blocks, all_weights):
            values = columns(vs_ref, head, low, high, frames)
            values = jnp.concatenate([values, jnp.ones_like(values)], 1)
            sums = jnp.dot(weights, values, preferred_element_type=jnp.float32)
            result = sums[:, :HEAD_DIM] / sums[:, HEAD_DIM:]
            for col in range(start, start + BLOCK_COLS):
                for row in range(rows):
                    low_row = row * FRAME_W + col * TILE_W
                    got = (col - start) * strip + row * TILE_W
                    lin_out_ref[low_row : low_row + TILE_W, :] = result[got : got + TILE_W, :]

    @pl.loop(0, heads)
    def _(head):
        more_frames = meta_ref[3 * head] > 0
        most = meta_ref[3 * head + 2] >= MOST_COLS

        @pl.when(more_frames & most)
        def _():
            one_head(head, (0.0, 1.0, away), MOST_COLS)

        for fewer in range(MOST_COLS):

            @pl.when(more_frames & (meta_ref[3 * head + 2] == fewer))
            def _(fewer=fewer):
                one_head(head, (0.0, 1.0, away), fewer)

        @pl.when(jnp.logical_not(more_frames))
        def _():
            one_head(head, (0.0,), MOST_COLS)

        lanes = pl.ds(pl.multiple_of(head * HEAD_DIM, HEAD_DIM), HEAD_DIM)
        for slot in range(slots):
            low = slot * chunk
            out_ref[slot, :, lanes] = lin_out_ref[low : low + slot_rows, :].astype(jnp.bfloat16)


def attend(zeros, meta, q, own, beside, away, chunk):
    slots, slot_rows, width = q.shape
    heads = width // HEAD_DIM
    tokens = slots * chunk
    lin_rows = padded(tokens + slot_rows - chunk)
    hbm = pl.BlockSpec(memory_space=pltpu.HBM)
    return pl.pallas_call(
        functools.partial(attend_kernel, chunk=chunk),
        out_shape=jax.ShapeDtypeStruct(q.shape, jnp.bfloat16),
        in_specs=[in_vmem(), in_smem()] + [in_vmem()] * 3 + [hbm],
        out_specs=in_vmem(),
        scratch_shapes=[
            pltpu.VMEM((heads, tokens, HEAD_DIM), jnp.bfloat16),
            pltpu.VMEM((heads, 3 * tokens, HEAD_DIM), jnp.bfloat16),
            pltpu.VMEM((heads, 3 * tokens, HEAD_DIM), jnp.bfloat16),
            pltpu.VMEM((lin_rows, HEAD_DIM), jnp.float32),
            pltpu.VMEM(beside.shape, beside.dtype),
            pltpu.SemaphoreType.DMA,
        ],
        compiler_params=params(16),
    )(zeros, meta, q, own, away, pltpu.with_memory_space_constraint(beside, pltpu.HBM))


def after_kernel(array_ref, out_ref):
    out_ref[...] = jnp.zeros_like(out_ref)


def after(array):
    return pl.pallas_call(
        after_kernel,
        out_shape=jax.ShapeDtypeStruct((8, HEAD_DIM), jnp.float32),
        in_specs=[pl.BlockSpec(memory_space=pl.ANY)],
        out_specs=in_vmem(),
        compiler_params=params(1),
        cost_estimate=pl.CostEstimate(flops=ORDER_FLOPS, bytes_accessed=0, transcendentals=0),
    )(array)


def turn(slab, slabs, groups):
    return jnp.where(slab >= slabs // 2, groups // 2, 0)


def exchange(array, pairs):
    groups, slabs = lax.axis_size("head"), lax.axis_size("slab")
    turned = [0 if slab < slabs // 2 else groups // 2 for slab in range(slabs)]
    both = [
        (a * groups + (group ^ turned[a]), b * groups + (group ^ turned[b]))
        for low, high in pairs
        for a, b in ((low, high), (high, low))
        for group in range(groups)
    ]
    return lax.ppermute(array, ("slab", "head"), both)


def swap(slots):
    return lax.all_to_all(slots, "head", split_axis=0, concat_axis=0)


def per_device(q_vals, k_vals, v_vals, q_scale, k_scale, v_scale, window):
    groups = lax.axis_size("head")
    slabs = lax.axis_size("slab")
    chunk = q_vals.shape[0]
    local_heads = q_scale.shape[1] // groups
    slab = lax.axis_index("slab")
    flip = turn(slab, slabs, groups).astype(jnp.int32)
    low = (lax.axis_index("head") ^ flip) * local_heads
    flip = flip.reshape(1)
    reach = lax.dynamic_slice_in_dim(window, low, local_heads, 0)
    linked = ((slab > 0) & (slab < slabs - 1)).astype(jnp.int32)
    meta = jnp.concatenate([reach.reshape(-1), linked.reshape(1)])
    kv, q = pack(flip, k_vals, v_vals, q_vals, k_scale, v_scale, q_scale)
    kv = swap(kv)
    away = exchange(kv, [(s, s + 1) for s in range(1, slabs - 1, 2)])
    beside = exchange(kv, [(s, s + 1) for s in range(0, slabs, 2)])
    q = swap(q)
    attended = attend(after(away), meta, q, kv, beside, away, chunk)
    return unpack(flip, swap(attended), chunk)


def solution(mesh):
    tokens = P(("slab", "head"), None)
    return jax.shard_map(
        per_device,
        mesh=mesh,
        in_specs=(tokens,) * 6 + (P(),),
        out_specs=tokens,
        check_vma=False,
    )
```

```python
import functools

import jax
import jax.numpy as jnp
from jax import lax
from jax.experimental import pallas as pl
from jax.experimental.pallas import tpu as pltpu
from jax.sharding import PartitionSpec as P

TILE_H = 5
TILE_W = 8
FRAME_W = 80
HEAD_DIM = 128
MASKED = -1e30
BLOCK_COLS = 2
MOST_COLS = 2
SCALE = 1.4426950408889634 / HEAD_DIM**0.5
ORDER_FLOPS = 2 * 10**10


def geometry(tokens):
    rows = tokens // FRAME_W
    return rows, FRAME_W // TILE_W, rows * TILE_W


def padded(rows):
    return -(-rows // 8) * 8


def params(mib):
    return pltpu.CompilerParams(vmem_limit_bytes=mib * 2**20)


def in_smem():
    return pl.BlockSpec(memory_space=pltpu.SMEM)


def in_vmem():
    return pl.BlockSpec(memory_space=pltpu.VMEM)


def pack_kernel(
    flip_ref, k_ref, v_ref, q_ref, ks_ref, vs_ref, qs_ref, kv_out, q_out, buf, scale_buf, sems
):
    groups, slot_rows, width = q_out.shape
    rows = k_ref.shape[0]
    heads = width // HEAD_DIM
    copies = [
        pltpu.make_async_copy(source, scale_buf.at[at], sems.at[at])
        for at, source in enumerate((ks_ref, vs_ref, qs_ref))
    ]
    copies += [
        pltpu.make_async_copy(source, buf.at[at], sems.at[3 + at])
        for at, source in enumerate((k_ref, v_ref, q_ref))
    ]
    for copy in copies:
        copy.start()
    for copy in copies[:-1]:
        copy.wait()
    blank = jnp.zeros((slot_rows - rows, HEAD_DIM), jnp.float32)
    scales = [scale_buf[at].astype(jnp.float32).T for at in range(3)]

    def scaled(at, index):
        vals = buf[at, :, index * HEAD_DIM : (index + 1) * HEAD_DIM]
        return vals.astype(jnp.float32) * scales[at][:, index : index + 1]

    for group in range(groups):
        indices = range(group * heads, (group + 1) * heads)
        stacked = [scaled(at, index) for index in indices for at in range(2)]
        slot = group ^ flip_ref[0]
        kv_out[slot] = jnp.concatenate(stacked, 0).astype(jnp.bfloat16)
    copies[-1].wait()
    for group in range(groups):
        slot = group ^ flip_ref[0]
        for head in range(heads):
            wide = scaled(2, group * heads + head)
            if slot_rows > rows:
                wide = jnp.concatenate([wide, blank], 0)
            low = head * HEAD_DIM
            q_out[slot, :, low : low + HEAD_DIM] = wide.astype(jnp.bfloat16)


def pack(flip, k_vals, v_vals, q_vals, k_scale, v_scale, q_scale):
    groups = lax.axis_size("head")
    rows, full = k_vals.shape
    width = full // groups
    slot_rows = padded(rows)
    operands = [
        pltpu.with_memory_space_constraint(x, pltpu.HBM)
        for x in (k_vals, v_vals, q_vals, k_scale.T, v_scale.T, q_scale.T)
    ]
    return pl.pallas_call(
        pack_kernel,
        out_shape=(
            jax.ShapeDtypeStruct((groups, 2 * rows * (width // HEAD_DIM), HEAD_DIM), jnp.bfloat16),
            jax.ShapeDtypeStruct((groups, slot_rows, width), jnp.bfloat16),
        ),
        in_specs=[in_smem()] + [pl.BlockSpec(memory_space=pltpu.HBM)] * 6,
        out_specs=(in_vmem(), in_vmem()),
        scratch_shapes=[
            pltpu.VMEM((3, rows, full), jnp.bfloat16),
            pltpu.VMEM((3, k_scale.shape[1], rows), jnp.bfloat16),
            pltpu.SemaphoreType.DMA((6,)),
        ],
        compiler_params=params(8),
    )(flip, *operands)


def unpack_kernel(flip_ref, in_ref, out_ref, buf, sems):
    groups, _, width = in_ref.shape
    rows = out_ref.shape[0]
    copies = []
    for group in range(groups):
        slot = in_ref[group ^ flip_ref[0]]
        buf[:, group * width : (group + 1) * width] = slot[:rows]
        if group % 2 == 1:
            cols = slice((group - 1) * width, (group + 1) * width)
            copy = pltpu.make_async_copy(
                buf.at[:, cols], out_ref.at[:, cols], sems.at[group // 2]
            )
            copy.start()
            copies.append(copy)
    for copy in copies:
        copy.wait()


def unpack(flip, slots, rows):
    groups, _, width = slots.shape
    return pl.pallas_call(
        unpack_kernel,
        out_shape=jax.ShapeDtypeStruct((rows, groups * width), jnp.bfloat16),
        in_specs=[in_smem(), in_vmem()],
        out_specs=pl.BlockSpec(memory_space=pltpu.HBM),
        scratch_shapes=[
            pltpu.VMEM((rows, groups * width), jnp.bfloat16),
            pltpu.SemaphoreType.DMA((groups // 2,)),
        ],
        compiler_params=params(4),
    )(flip, slots)


def tokens_by_eight(slots, base, chunk):
    first_half = lax.broadcasted_iota(jnp.int32, (TILE_W, HEAD_DIM), 0) < TILE_W // 2
    half = TILE_W // 2
    turned = {}

    def aligned(slot, low):
        return slots[slot][low : low + TILE_W, :]

    def halves_swapped(slot, low):
        if (slot, low) not in turned:
            turned[slot, low] = pltpu.roll(aligned(slot, low), half, 0)
        return turned[slot, low]

    def upper(slot, low):
        return aligned(slot, low) if low % TILE_W == 0 else halves_swapped(slot, low - half)

    def lower(slot, low):
        return halves_swapped(slot, low) if low % TILE_W == 0 else aligned(slot, low - half)

    def eight(slot, low):
        if low % TILE_W == 0:
            return aligned(slot, low)
        return jnp.where(first_half, upper(slot, low), lower(slot, low + half))

    full = chunk // TILE_W
    for slot in range(0, len(slots), 2):
        for at in range(full):
            yield eight(slot, base + at * TILE_W)
        yield jnp.where(first_half, upper(slot, base + full * TILE_W), lower(slot + 1, base))
        for at in range(full):
            yield eight(slot + 1, base + half + at * TILE_W)


def by_columns(slots, base, chunk):
    cols = FRAME_W // TILE_W
    groups = list(tokens_by_eight(slots, base, chunk))
    return [jnp.concatenate(groups[col::cols], 0) for col in range(cols)]


def blocks(cols, reach):
    for start in range(0, cols, BLOCK_COLS):
        yield start, max(0, start - reach), min(cols, start + BLOCK_COLS + reach)


def shifts(block, strip, rows, frames, frame_reach, row_reach, col_reach):
    start, low_col, high_col = block
    span = len(frames)
    half = strip * TILE_H // rows
    keys = (high_col - low_col) * span * strip
    at = lax.broadcasted_iota(jnp.int32, (1, keys), 1).astype(jnp.float32)
    key_col = jnp.floor((at + 0.5) * (1.0 / (span * strip)))
    rest = at - key_col * (span * strip)
    key_frame = jnp.floor((rest + 0.5) * (1.0 / strip))
    rest = rest - key_frame * strip
    key_row = jnp.floor((rest + 0.5) * (1.0 / half))
    gap = jnp.zeros_like(at)
    for frame, far in enumerate(frames):
        gap = jnp.where(key_frame == frame, far, gap)
    frame_ok = gap <= frame_reach
    for col in range(start, start + BLOCK_COLS):
        col_ok = frame_ok & (jnp.abs(key_col - (col - low_col)) <= col_reach)
        for row in range(rows // TILE_H):
            row_ok = jnp.abs(key_row - row) <= row_reach
            low = (col - start) * strip + row * half
            yield slice(low, low + half), jnp.where(col_ok & row_ok, 0.0, MASKED)


def attend_kernel(
    zeros_ref, meta_ref, q_ref, own_ref, away_ref, beside_hbm, out_ref, qs_ref, ks_ref, vs_ref, lin_out_ref,
    beside_ref, sem, *, chunk,
):
    slots, slot_rows, width = out_ref.shape
    heads = width // HEAD_DIM
    tokens = slots * chunk
    rows, cols, strip = geometry(tokens)
    span = 3
    copy = pltpu.make_async_copy(beside_hbm, beside_ref, sem)
    copy.start()
    lin_out_ref[tokens:, :] = zeros_ref[: lin_out_ref.shape[0] - tokens, :]
    away = jnp.where(meta_ref[3 * heads] > 0, 1.0, 2.0)

    for head in range(heads):
        lanes = slice(head * HEAD_DIM, (head + 1) * HEAD_DIM)
        taken = [q_ref[slot, :, lanes].astype(jnp.float32) for slot in range(slots)]
        for col, part in enumerate(by_columns(taken, 0, chunk)):
            qs_ref[head, col * strip : (col + 1) * strip, :] = part.astype(jnp.bfloat16)

    def by_head(frame, source, head):
        taken = [source[slot].astype(jnp.float32) for slot in range(slots)]
        for at, target in enumerate((ks_ref, vs_ref)):
            for col, part in enumerate(by_columns(taken, (2 * head + at) * chunk, chunk)):
                low = (col * span + frame) * strip
                target[head, low : low + strip, :HEAD_DIM] = part.astype(jnp.bfloat16)

    for head in range(heads):
        by_head(0, own_ref, head)
    for frame, source in ((2, away_ref), (1, beside_ref)):
        if source is beside_ref:
            copy.wait()
        for head in range(heads):

            @pl.when(meta_ref[3 * head] > 0)
            def _(frame=frame, source=source, head=head):
                by_head(frame, source, head)

    def columns(ref, head, low, high, frames):
        if len(frames) == span:
            return ref[head, low * span * strip : high * span * strip, :]
        first = [col * span * strip for col in range(low, high)]
        return jnp.concatenate([ref[head, at : at + strip, :] for at in first], 0)

    def one_head(head, frames, most_cols):
        reach = [meta_ref[3 * head + i].astype(jnp.float32) for i in range(3)]
        all_blocks = list(blocks(cols, most_cols))
        all_scores = [
            lax.dot_general(
                qs_ref[head, start * strip : (start + BLOCK_COLS) * strip, :],
                columns(ks_ref, head, low, high, frames),
                (((1,), (1,)), ((), ())),
                preferred_element_type=jnp.float32,
            )
            for start, low, high in all_blocks
        ]
        all_weights = []
        for block, scores in zip(all_blocks, all_scores):
            weights = []
            for mine, shift in shifts(block, strip, rows, frames, *reach):
                masked = scores[mine, :] + shift
                top = jnp.max(masked, axis=1, keepdims=True)
                weights.append(jnp.exp2((masked - top) * SCALE))
            all_weights.append(jnp.concatenate(weights, 0).astype(jnp.bfloat16))
        for (start, low, high), weights in zip(all_blocks, all_weights):
            values = columns(vs_ref, head, low, high, frames)
            values = jnp.concatenate([values, jnp.ones_like(values)], 1)
            sums = jnp.dot(weights, values, preferred_element_type=jnp.float32)
            result = sums[:, :HEAD_DIM] / sums[:, HEAD_DIM:]
            for col in range(start, start + BLOCK_COLS):
                for row in range(rows):
                    low_row = row * FRAME_W + col * TILE_W
                    got = (col - start) * strip + row * TILE_W
                    lin_out_ref[low_row : low_row + TILE_W, :] = result[got : got + TILE_W, :]

    @pl.loop(0, heads)
    def _(head):
        more_frames = meta_ref[3 * head] > 0
        most = meta_ref[3 * head + 2] >= MOST_COLS

        @pl.when(more_frames & most)
        def _():
            one_head(head, (0.0, 1.0, away), MOST_COLS)

        for fewer in range(MOST_COLS):

            @pl.when(more_frames & (meta_ref[3 * head + 2] == fewer))
            def _(fewer=fewer):
                one_head(head, (0.0, 1.0, away), fewer)

        @pl.when(jnp.logical_not(more_frames))
        def _():
            one_head(head, (0.0,), MOST_COLS)

        lanes = pl.ds(pl.multiple_of(head * HEAD_DIM, HEAD_DIM), HEAD_DIM)
        for slot in range(slots):
            low = slot * chunk
            out_ref[slot, :, lanes] = lin_out_ref[low : low + slot_rows, :].astype(jnp.bfloat16)


def attend(zeros, meta, q, own, beside, away, chunk):
    slots, slot_rows, width = q.shape
    heads = width // HEAD_DIM
    tokens = slots * chunk
    lin_rows = padded(tokens + slot_rows - chunk)
    hbm = pl.BlockSpec(memory_space=pltpu.HBM)
    return pl.pallas_call(
        functools.partial(attend_kernel, chunk=chunk),
        out_shape=jax.ShapeDtypeStruct(q.shape, jnp.bfloat16),
        in_specs=[in_vmem(), in_smem()] + [in_vmem()] * 3 + [hbm],
        out_specs=in_vmem(),
        scratch_shapes=[
            pltpu.VMEM((heads, tokens, HEAD_DIM), jnp.bfloat16),
            pltpu.VMEM((heads, 3 * tokens, HEAD_DIM), jnp.bfloat16),
            pltpu.VMEM((heads, 3 * tokens, HEAD_DIM), jnp.bfloat16),
            pltpu.VMEM((lin_rows, HEAD_DIM), jnp.float32),
            pltpu.VMEM(beside.shape, beside.dtype),
            pltpu.SemaphoreType.DMA,
        ],
        compiler_params=params(16),
    )(zeros, meta, q, own, away, pltpu.with_memory_space_constraint(beside, pltpu.HBM))


def after_kernel(array_ref, out_ref):
    out_ref[...] = jnp.zeros_like(out_ref)


def after(array):
    return pl.pallas_call(
        after_kernel,
        out_shape=jax.ShapeDtypeStruct((8, HEAD_DIM), jnp.float32),
        in_specs=[pl.BlockSpec(memory_space=pl.ANY)],
        out_specs=in_vmem(),
        compiler_params=params(1),
        cost_estimate=pl.CostEstimate(flops=ORDER_FLOPS, bytes_accessed=0, transcendentals=0),
    )(array)


def turn(slab, slabs, groups):
    return jnp.where(slab >= slabs // 2, groups // 2, 0)


def exchange(array, pairs):
    groups, slabs = lax.axis_size("head"), lax.axis_size("slab")
    turned = [0 if slab < slabs // 2 else groups // 2 for slab in range(slabs)]
    both = [
        (a * groups + (group ^ turned[a]), b * groups + (group ^ turned[b]))
        for low, high in pairs
        for a, b in ((low, high), (high, low))
        for group in range(groups)
    ]
    return lax.ppermute(array, ("slab", "head"), both)


def swap(slots):
    return lax.all_to_all(slots, "head", split_axis=0, concat_axis=0)


def per_device(q_vals, k_vals, v_vals, q_scale, k_scale, v_scale, window):
    groups = lax.axis_size("head")
    slabs = lax.axis_size("slab")
    chunk = q_vals.shape[0]
    local_heads = q_scale.shape[1] // groups
    slab = lax.axis_index("slab")
    flip = turn(slab, slabs, groups).astype(jnp.int32)
    low = (lax.axis_index("head") ^ flip) * local_heads
    flip = flip.reshape(1)
    reach = lax.dynamic_slice_in_dim(window, low, local_heads, 0)
    linked = ((slab > 0) & (slab < slabs - 1)).astype(jnp.int32)
    meta = jnp.concatenate([reach.reshape(-1), linked.reshape(1)])
    kv, q = pack(flip, k_vals, v_vals, q_vals, k_scale, v_scale, q_scale)
    kv = swap(kv)
    away = exchange(kv, [(s, s + 1) for s in range(1, slabs - 1, 2)])
    beside = exchange(kv, [(s, s + 1) for s in range(0, slabs, 2)])
    q = swap(q)
    attended = attend(after(away), meta, q, kv, beside, away, chunk)
    return unpack(flip, swap(attended), chunk)


def solution(mesh):
    tokens = P(("slab", "head"), None)
    return jax.shard_map(
        per_device,
        mesh=mesh,
        in_specs=(tokens,) * 6 + (P(),),
        out_specs=tokens,
        check_vma=False,
    )
```
